32 devices in a mesh: dp: 8 (over z, x), expert: 4 (over y, core).
Axes of the slice: x: 2, y: 2, z: 4, core: 2. Of those that a mesh axis runs over, the one named last changes fastest.
Arguments:
- tokens: bfloat16 [16384, 1024], P(('dp', 'expert')), may hold values from -6 to 6
- block_expert: int32 [128], P(('dp', 'expert')), may hold values from 0 to 31, as said below
- gate_weight: bfloat16 [32, 1024, 384], P('expert'), may hold values from -0.1875 to 0.1875
- up_weight: bfloat16 [32, 1024, 384], P('expert'), may hold values from -0.1875 to 0.1875
Outputs:
- gram_factor: float32 [32, 384, 384], P('expert', 'dp')
The draws below stay inside these ranges and needn't reach their ends.
Inputs may be any that keep to these rules, and one draw needn't show every extreme that they name: `block_expert`: expert e is held by index e // 8 of the expert axis. Among the 4 blocks of one device, at most 1 name experts of any one index of the expert axis; in every group of devices along the expert axis, one index of the expert axis receives exactly 1 block from every device of the group.
All inputs are finite; a program needn't handle non-finite values.
Results may differ from the reference program's by a relative error of at most 0.0031.
Values may be sent and summed in bfloat16 or wider, within the bound.
A program may use at most 128 MiB of HBM per device.

```python
import jax
import jax.numpy as jnp
from jax import lax

D = 1024
FF = 384
EXP_DEV = 8
BLOCK = 128
BLK_DEV = 4
CAP = 1
EXPERTS = 32
TOKENS = 16384
BLOCKS = 128
NORM_ROWS = 512
N_DP = 8
N_EXPERT = 4


def draw_block_expert(key, part):
    devices = N_DP * N_EXPERT
    remaining = BLK_DEV - CAP
    spare_slots = (N_EXPERT - 1) * CAP
    key_hot, key_pick, key_local, key_order = jax.random.split(key, 4)
    hot_owner = jax.random.randint(key_hot, (N_DP, 1), 0, N_EXPERT)
    hot_owner = jnp.broadcast_to(hot_owner, (N_DP, N_EXPERT)).reshape(devices, 1)
    scores = jax.random.randint(key_pick, (devices, spare_slots), 0, 1 << 20) * spare_slots + jnp.arange(spare_slots)
    chosen = jnp.argsort(scores, axis=1)[:, :remaining]
    others = (hot_owner + 1 + chosen // CAP) % N_EXPERT
    owners_all = jnp.concatenate([jnp.broadcast_to(hot_owner, (devices, CAP)), others], axis=1)
    local_expert = jax.random.randint(key_local, (devices, BLK_DEV), 0, EXP_DEV)
    order_scores = jax.random.randint(key_order, (devices, BLK_DEV), 0, 1 << 20) * BLK_DEV + jnp.arange(BLK_DEV)
    shuffle = jnp.argsort(order_scores, axis=1)
    owners_all = jnp.take_along_axis(owners_all, shuffle, axis=1)
    return (owners_all * EXP_DEV + local_expert).reshape(-1).astype(jnp.int32)


def levels(stream_key, extent, pieces, low, high):
    def one(position, blocks):
        draws = jax.random.uniform(jax.random.fold_in(jax.random.fold_in(stream_key, 6), position), (blocks,), jnp.float32, low / len(pieces), high / len(pieces))
        return jnp.repeat(jnp.exp(draws), extent[position] // blocks).reshape((-1,) + (1,) * (len(extent) - position - 1))

    level = one(*pieces[0])
    for cut in pieces[1:]:
        level = level * one(*cut)
    return level


def bell_draw(stream_key, shape, deviation, bound, cuts=(), kind=jnp.bfloat16):
    result = jax.random.normal(stream_key, shape, jnp.float32) * deviation
    if len(cuts) > 0:
        result = levels(stream_key, shape, cuts, -0.22, 0.18) * result
    return jnp.clip(result, min=-bound, max=bound).astype(kind)


def setup_inputs(seed: int = 0) -> dict:
    key_list = jax.random.split(jax.random.key(seed), 5)
    tokens = bell_draw(key_list[0], (TOKENS, D), 1.0, 6.0, ((0, 32),))
    block_expert = draw_block_expert(jax.random.fold_in(key_list[4], 71), 0)
    gate_weight = bell_draw(key_list[2], (EXPERTS, D, FF), D ** -0.5, 0.1875, ((0, 4),))
    up_weight = bell_draw(key_list[3], (EXPERTS, D, FF), D ** -0.5, 0.1875, ((0, 4),))
    return dict(tokens=tokens, block_expert=block_expert, gate_weight=gate_weight, up_weight=up_weight)


RIDGE = 0.05

def reference(tokens, block_expert, gate_weight, up_weight):
    blocks = tokens.reshape(BLOCKS, BLOCK, D)

    def accumulate(gram_sum, entry):
        rows_in, expert = entry
        gate_matrix = lax.dynamic_index_in_dim(gate_weight, expert, 0, keepdims=False)
        up_matrix = lax.dynamic_index_in_dim(up_weight, expert, 0, keepdims=False)
        gate_proj = jnp.dot(rows_in.astype(jnp.float32), gate_matrix.astype(jnp.float32), preferred_element_type=jnp.float32)
        up_proj = jnp.dot(rows_in.astype(jnp.float32), up_matrix.astype(jnp.float32), preferred_element_type=jnp.float32)
        hidden = (jax.nn.silu(gate_proj) * up_proj).astype(jnp.bfloat16)
        product = jnp.dot(hidden.T.astype(jnp.float32), hidden.astype(jnp.float32), preferred_element_type=jnp.float32)
        current = lax.dynamic_index_in_dim(gram_sum, expert, 0, keepdims=False)
        gram_sum = lax.dynamic_update_index_in_dim(gram_sum, current + product, expert, 0)
        return (gram_sum, None)
    start_sum = jnp.zeros((EXPERTS, FF, FF), jnp.float32)
    gram_sum, unused = lax.scan(accumulate, start_sum, (blocks, block_expert.astype(jnp.int32)))
    gram = gram_sum * (1.0 / NORM_ROWS) + RIDGE * jnp.eye(FF, dtype=jnp.float32)
    lower_part = jnp.linalg.cholesky(gram)
    return jnp.swapaxes(lower_part, 1, 2)
```

```python
import functools

import jax
import jax.numpy as jnp
from jax import lax
from jax.experimental import pallas as pl
from jax.experimental.pallas import tpu as pltpu
from jax.sharding import PartitionSpec as P

BLOCK = 128
RIDGE = 0.05
PANEL = 8
LANES = 128
MESH = pl.DeviceIdType.MESH
HIGHEST = lax.Precision.HIGHEST


def flip(index, bits, count):
    out = 0
    bit = 1
    while bit < count:
        digit = (index // bit) % 2
        out = out + bit * ((digit + 1) % 2 if bits & bit else digit)
        bit *= 2
    return out


def ring_place(dp, count):
    row, side = dp // 2, dp % 2
    return row + side * (count - 1 - 2 * row)


def ring_index(place, count):
    late = place // (count // 2)
    return (1 - late) * 2 * place + late * (2 * (count - 1 - place) + 1)


def gram_kernel(
    owners, replicas, experts, scale,
    expert_ref, tokens_ref, gate_hbm, up_hbm, gram_ref,
    gate_w, up_w, outgoing, arrived, id_out, id_in, id_smem, id_tile, id_ring,
    hidden, ring, w_sem, tok_sem, id_sem, small_sem, ring_sem, idr_sem,
):
    dp = lax.axis_index("dp")
    member = lax.axis_index("expert")
    width = gram_ref.shape[0]
    blocks_dev = expert_ref.shape[0]
    place = ring_place(dp, replicas)
    right = ring_index((place + 1) % replicas, replicas)
    left = ring_index((place + replicas - 1) % replicas, replicas)
    mine = dp // max(1, replicas // experts)

    load_gate = pltpu.make_async_copy(gate_hbm, gate_w, w_sem.at[0])
    load_up = pltpu.make_async_copy(up_hbm, up_w, w_sem.at[1])
    load_gate.start()
    load_up.start()

    barrier = pltpu.get_barrier_semaphore()
    for r in range(1, owners):
        pl.semaphore_signal(
            barrier, inc=1, device_id=(dp, flip(member, r, owners)), device_id_type=MESH
        )
    for side in (left, right):
        pl.semaphore_signal(barrier, inc=1, device_id=(side, member), device_id_type=MESH)

    picks = []
    for r in range(owners):
        target = flip(member, r, owners)
        index = jnp.int32(0)
        local = jnp.int32(-1)
        for b in range(blocks_dev):
            named = expert_ref[b]
            hit = named // experts == target
            index = jnp.where(hit, b, index)
            local = jnp.where(hit, named % experts, local)
        picks.append((index, local))
        id_out[r] = jnp.full((8, LANES), local, jnp.int32)
    pl.semaphore_wait(barrier, owners + 1)

    def remote(src, dst, sems, device):
        return pltpu.make_async_remote_copy(
            src_ref=src, dst_ref=dst, send_sem=sems.at[0], recv_sem=sems.at[1],
            device_id=device, device_id_type=MESH,
        )

    sent = []
    id_copies = [None]
    token_copies = [None]
    for r in range(1, owners):
        device = (dp, flip(member, r, owners))
        copy = remote(id_out.at[r], id_in.at[r], id_sem.at[r], device)
        copy.start()
        id_copies.append(copy)
        sent.append(copy)
    for r in range(1, owners):
        device = (dp, flip(member, r, owners))
        outgoing[r] = tokens_ref[picks[r][0]]
        copy = remote(outgoing.at[r], arrived.at[r], tok_sem.at[r], device)
        copy.start()
        token_copies.append(copy)
        sent.append(copy)

    locals_in = [picks[0][1]]
    for r in range(1, owners):
        id_copies[r].wait_recv()
        small = pltpu.make_async_copy(id_in.at[r], id_smem.at[r], small_sem.at[r])
        small.start()
        small.wait()
        locals_in.append(id_smem[r, 0, 0])
    for r in range(owners):
        id_tile[r * 16 : r * 16 + 16, :] = jnp.full(
            (16, LANES), locals_in[r].astype(jnp.float32), jnp.float32
        ).astype(jnp.bfloat16)

    def hops(direction, block):
        longer = replicas // 2
        first = block < owners // 2
        return longer if first == (direction == 0) else replicas - 1 - longer

    longest = replicas // 2
    peers = ((right, member), (left, member))
    id_moves = {}

    def send_ids(direction, hop):
        src = id_tile if hop == 1 else id_ring.at[direction, hop - 2]
        copy = remote(src, id_ring.at[direction, hop - 1], idr_sem.at[direction, hop - 1], peers[direction])
        copy.start()
        id_moves[direction, hop] = copy
        sent.append(copy)

    moves = {}

    def send_block(direction, hop, block):
        if hop > hops(direction, block):
            return
        src = hidden.at[block] if hop == 1 else ring.at[direction, hop - 2, block]
        copy = remote(
            src, ring.at[direction, hop - 1, block], ring_sem.at[direction, hop - 1, block],
            peers[direction],
        )
        copy.start()
        moves[direction, hop, block] = copy
        sent.append(copy)

    def add_gram(rows, ids):
        match = (ids.astype(jnp.float32) == mine.astype(jnp.float32)).astype(jnp.float32)
        match = jnp.concatenate([match] * (width // LANES), axis=1)
        kept = (rows.astype(jnp.float32) * match).astype(jnp.bfloat16)
        gram_ref[...] += lax.dot_general(
            kept, rows, (((0,), (0,)), ((), ())), preferred_element_type=jnp.float32
        )

    for direction in range(2):
        send_ids(direction, 1)
    gram_ref[...] = jnp.zeros_like(gram_ref)
    load_gate.wait()
    load_up.wait()

    events = []
    for b in range(owners):
        ready = 0.0 if b == 0 else (0.5 if b == 1 else 4.0 * (b - 1) - 0.5)
        events.append((ready, 0, -1, b))
        for direction in range(2):
            for hop in range(1, hops(direction, b) + 1):
                events.append((ready + 4.0 * hop, hop, direction, b))
    events.sort()
    for _, hop, direction, b in events:
        if hop == 0:
            if b > 0:
                token_copies[b].wait_recv()
                rows_in = arrived[b]
            else:
                rows_in = tokens_ref[picks[0][0]]
            which = jnp.maximum(locals_in[b], 0)
            gate = jnp.dot(rows_in, gate_w[which], preferred_element_type=jnp.float32)
            up = jnp.dot(rows_in, up_w[which], preferred_element_type=jnp.float32)
            hidden[b] = (gate / (1.0 + jnp.exp(-gate)) * up).astype(jnp.bfloat16)
            for d in range(2):
                send_block(d, 1, b)
            add_gram(hidden[b], id_tile[b * 16 : b * 16 + 1, :])
        else:
            if (direction, hop) in id_moves:
                id_moves.pop((direction, hop)).wait_recv()
                if hop < longest:
                    send_ids(direction, hop + 1)
            moves[direction, hop, b].wait_recv()
            send_block(direction, hop + 1, b)
            add_gram(ring[direction, hop - 1, b], id_ring[direction, hop - 1, b * 16 : b * 16 + 1, :])
    for copy in sent:
        copy.wait_send()
    row = lax.broadcasted_iota(jnp.int32, (width, width), 0)
    col = lax.broadcasted_iota(jnp.int32, (width, width), 1)
    gram_ref[...] = gram_ref[...] * scale + jnp.where(row == col, RIDGE, 0.0)


def grams(tokens, block_expert, gate_weight, up_weight):
    owners = lax.axis_size("expert")
    replicas = lax.axis_size("dp")
    experts, model, width = gate_weight.shape
    mean_rows = tokens.shape[0] * replicas // experts
    longest = replicas // 2
    bf16 = jnp.bfloat16
    vmem = pl.BlockSpec(memory_space=pltpu.VMEM)
    anywhere = pl.BlockSpec(memory_space=pl.ANY)
    dma = pltpu.SemaphoreType.DMA
    return pl.pallas_call(
        functools.partial(gram_kernel, owners, replicas, experts, 1.0 / mean_rows),
        out_shape=jax.ShapeDtypeStruct((width, width), jnp.float32),
        in_specs=[pl.BlockSpec(memory_space=pltpu.SMEM), vmem, anywhere, anywhere],
        out_specs=vmem,
        scratch_shapes=[
            pltpu.VMEM((experts, model, width), bf16),
            pltpu.VMEM((experts, model, width), bf16),
            pltpu.VMEM((owners, BLOCK, model), bf16),
            pltpu.VMEM((owners, BLOCK, model), bf16),
            pltpu.VMEM((owners, 8, LANES), jnp.int32),
            pltpu.VMEM((owners, 8, LANES), jnp.int32),
            pltpu.SMEM((owners, 8, LANES), jnp.int32),
            pltpu.VMEM((owners * 16, LANES), bf16),
            pltpu.VMEM((2, longest, owners * 16, LANES), bf16),
            pltpu.VMEM((owners, BLOCK, width), bf16),
            pltpu.VMEM((2, longest, owners, BLOCK, width), bf16),
            dma((2,)),
            dma((owners, 2)),
            dma((owners, 2)),
            dma((owners,)),
            dma((2, longest, owners, 2)),
            dma((2, longest, 2)),
        ],
        compiler_params=pltpu.CompilerParams(
            collective_id=0, has_side_effects=True, vmem_limit_bytes=52 * 1024 * 1024
        ),
        name="grams",
    )(block_expert, tokens.reshape(-1, BLOCK, model), gate_weight, up_weight)


def eliminate(tile, rows_done):
    size = tile.shape[0]
    count = size // PANEL
    halves = tile.shape[1] // LANES

    def spread(vector, lane):
        return jnp.broadcast_to(vector[:, lane : lane + 1], (PANEL, LANES))

    def down(vector, sub):
        return jnp.broadcast_to(vector[sub : sub + 1, :], (PANEL, LANES))

    groups = [
        [tile[g * PANEL : (g + 1) * PANEL, h * LANES : (h + 1) * LANES] for h in range(halves)]
        for g in range(count)
    ]
    for p in range(count):
        panel = groups[p]
        cols = [spread(panel[0], p * PANEL + k) for k in range(PANEL)]
        small = [[down(cols[k], i) if i >= k else None for k in range(PANEL)] for i in range(PANEL)]
        inverse = []
        low = [[None] * PANEL for _ in range(PANEL)]
        for k in range(PANEL):
            inv = lax.rsqrt(small[k][k])
            inverse.append(inv)
            for i in range(k + 1, PANEL):
                low[i][k] = small[i][k] * inv
            for i in range(k + 1, PANEL):
                for m in range(k + 1, i + 1):
                    small[i][m] = small[i][m] - low[i][k] * low[m][k]
        rows = []
        for k in range(PANEL):
            parts = []
            for h in range(halves):
                value = down(panel[h], k)
                for m in range(k):
                    value = value - low[k][m] * rows[m][h]
                parts.append(value * inverse[k])
            rows.append(parts)
            for h in range(halves):
                rows_done[p * PANEL + k : p * PANEL + k + 1, h * LANES : (h + 1) * LANES] = parts[h][0:1, :]
        for g in range(p + 1, count):
            weights = []
            for k in range(PANEL):
                value = spread(groups[g][0], p * PANEL + k)
                for m in range(k):
                    value = value - low[k][m] * weights[m]
                weights.append(value * inverse[k])
            for h in range(halves):
                value = groups[g][h]
                for k in range(PANEL):
                    value = value - weights[k] * rows[k][h]
                groups[g][h] = value


def factor_kernel(gram_ref, factor_ref, work, tile, done):
    width = gram_ref.shape[0]
    work[...] = gram_ref[...]
    row = lax.broadcasted_iota(jnp.int32, (LANES, LANES), 0)
    col = lax.broadcasted_iota(jnp.int32, (LANES, LANES), 1)

    def step(b, carry):
        at = pl.ds(pl.multiple_of(b * LANES, LANES), LANES)
        tile[:, :LANES] = work[at, at]
        tile[:, LANES:] = jnp.where(row == col, 1.0, 0.0)
        eliminate(tile, done)
        wide = jnp.dot(
            done[:, LANES:], work[at, :], precision=HIGHEST, preferred_element_type=jnp.float32
        )
        across = lax.broadcasted_iota(jnp.int32, wide.shape, 1) - b * LANES
        factor_ref[at, :] = jnp.where(across >= LANES, wide, 0.0)
        factor_ref[at, at] = jnp.where(row <= col, done[:, :LANES], 0.0)

        @pl.when(b + 1 < width // LANES)
        def _():
            work[...] -= lax.dot_general(
                wide, wide, (((0,), (0,)), ((), ())), precision=HIGHEST,
                preferred_element_type=jnp.float32,
            )

        return carry

    lax.fori_loop(0, width // LANES, step, 0)


def factored(gram):
    width = gram.shape[0]
    vmem = pl.BlockSpec(memory_space=pltpu.VMEM)
    return pl.pallas_call(
        factor_kernel,
        out_shape=jax.ShapeDtypeStruct((width, width), jnp.float32),
        in_specs=[vmem],
        out_specs=vmem,
        scratch_shapes=[
            pltpu.VMEM((width, width), jnp.float32),
            pltpu.VMEM((LANES, 2 * LANES), jnp.float32),
            pltpu.VMEM((LANES, 2 * LANES), jnp.float32),
        ],
        compiler_params=pltpu.CompilerParams(vmem_limit_bytes=16 * 1024 * 1024),
        name="factored",
    )(gram)


def spread_kernel(replicas, copies, factor_ref, out_ref, landed, sems):
    dp = lax.axis_index("dp")
    member = lax.axis_index("expert")
    rows = out_ref.shape[1]
    barrier = pltpu.get_barrier_semaphore()
    offsets = list(range(copies, replicas, copies))
    for r in offsets:
        pl.semaphore_signal(
            barrier, inc=1, device_id=((dp + r) % replicas, member), device_id_type=MESH
        )
    pl.semaphore_wait(barrier, len(offsets))
    sent = []
    for n, r in enumerate(offsets):
        to = (dp + r) % replicas
        copy = pltpu.make_async_remote_copy(
            src_ref=factor_ref.at[pl.ds(pl.multiple_of(to * rows, 8), rows), :],
            dst_ref=landed.at[n],
            send_sem=sems.at[n, 0],
            recv_sem=sems.at[n, 1],
            device_id=(to, member),
            device_id_type=MESH,
        )
        copy.start()
        sent.append(copy)
    out_ref[dp // copies] = factor_ref[pl.ds(pl.multiple_of(dp * rows, 8), rows), :]
    for n, r in enumerate(offsets):
        sent[n].wait_recv()
        origin = (dp + replicas - r) % replicas
        out_ref[origin // copies] = landed[n]
    for copy in sent:
        copy.wait_send()


def spread_rows(factor, experts):
    replicas = lax.axis_size("dp")
    copies = replicas // experts
    width = factor.shape[0]
    rows = width // replicas
    vmem = pl.BlockSpec(memory_space=pltpu.VMEM)
    return pl.pallas_call(
        functools.partial(spread_kernel, replicas, copies),
        out_shape=jax.ShapeDtypeStruct((experts, rows, width), jnp.float32),
        in_specs=[vmem],
        out_specs=vmem,
        scratch_shapes=[
            pltpu.VMEM((experts - 1, rows, width), jnp.float32),
            pltpu.SemaphoreType.DMA((experts - 1, 2)),
        ],
        compiler_params=pltpu.CompilerParams(
            collective_id=1, has_side_effects=True, vmem_limit_bytes=16 * 1024 * 1024
        ),
        name="spread_rows",
    )(factor)


def on_device(tokens, block_expert, gate_weight, up_weight):
    gram = grams(tokens, block_expert, gate_weight, up_weight)
    return spread_rows(factored(gram), gate_weight.shape[0])


def solution(mesh):
    placed = (
        P(("dp", "expert"), None),
        P(("dp", "expert")),
        P("expert", None, None),
        P("expert", None, None),
    )
    return jax.shard_map(
        on_device, mesh=mesh, in_specs=placed, out_specs=P("expert", "dp", None), check_vma=False
    )
```

```python
import functools
import heapq

import jax
import jax.numpy as jnp
from jax import lax
from jax.experimental import pallas as pl
from jax.experimental.pallas import tpu as pltpu
from jax.sharding import PartitionSpec as P

BLOCK = 128
RIDGE = 0.05
PANEL = 8
LANES = 128
MESH = pl.DeviceIdType.MESH
HIGHEST = lax.Precision.HIGHEST


def flip(index, bits, count):
    out = 0
    bit = 1
    while bit < count:
        digit = (index // bit) % 2
        out = out + bit * ((digit + 1) % 2 if bits & bit else digit)
        bit *= 2
    return out


def ready_time(block):
    return (0.0, 0.7, 6.0, 7.5)[block] if block < 4 else 2.0 * block


def ring_place(dp, count):
    row, side = dp // 2, dp % 2
    return row + side * (count - 1 - 2 * row)


def ring_index(place, count):
    late = place // (count // 2)
    return (1 - late) * 2 * place + late * (2 * (count - 1 - place) + 1)


def gram_kernel(
    owners, replicas, experts, scale,
    expert_ref, tokens_hbm, gate_hbm, up_hbm, gram_ref,
    tokens_ref, gate_w, up_w, outgoing, arrived, id_out, id_in, id_smem, id_tile, id_ring,
    hidden, ring, w_sem, tok_sem, id_sem, small_sem, ring_sem, idr_sem,
):
    dp = lax.axis_index("dp")
    member = lax.axis_index("expert")
    width = gram_ref.shape[0]
    blocks_dev = expert_ref.shape[0]
    place = ring_place(dp, replicas)
    right = ring_index((place + 1) % replicas, replicas)
    left = ring_index((place + replicas - 1) % replicas, replicas)
    mine = dp // max(1, replicas // experts)

    load_gate = pltpu.make_async_copy(gate_hbm, gate_w, w_sem.at[0])
    load_up = pltpu.make_async_copy(up_hbm, up_w, w_sem.at[1])
    load_tokens = pltpu.make_async_copy(tokens_hbm, tokens_ref, w_sem.at[2])
    load_tokens.start()
    load_gate.start()
    load_up.start()

    barrier = pltpu.get_barrier_semaphore()
    for r in range(1, owners):
        pl.semaphore_signal(
            barrier, inc=1, device_id=(dp, flip(member, r, owners)), device_id_type=MESH
        )
    for side in (left, right):
        pl.semaphore_signal(barrier, inc=1, device_id=(side, member), device_id_type=MESH)

    picks = []
    for r in range(owners):
        target = flip(member, r, owners)
        index = jnp.int32(0)
        local = jnp.int32(-1)
        for b in range(blocks_dev):
            named = expert_ref[b]
            hit = named // experts == target
            index = jnp.where(hit, b, index)
            local = jnp.where(hit, named % experts, local)
        picks.append((index, local))
        id_out[r] = jnp.full((8, LANES), local, jnp.int32)
    pl.semaphore_wait(barrier, owners + 1)

    def remote(src, dst, sems, device):
        return pltpu.make_async_remote_copy(
            src_ref=src, dst_ref=dst, send_sem=sems.at[0], recv_sem=sems.at[1],
            device_id=device, device_id_type=MESH,
        )

    sent = []
    id_copies = [None]
    token_copies = [None]
    for r in range(1, owners):
        device = (dp, flip(member, r, owners))
        copy = remote(id_out.at[r], id_in.at[r], id_sem.at[r], device)
        copy.start()
        id_copies.append(copy)
        sent.append(copy)
    load_tokens.wait()
    for r in range(1, owners):
        device = (dp, flip(member, r, owners))
        outgoing[r] = tokens_ref[picks[r][0]]
        copy = remote(outgoing.at[r], arrived.at[r], tok_sem.at[r], device)
        copy.start()
        token_copies.append(copy)
        sent.append(copy)

    locals_in = [picks[0][1]]
    for r in range(1, owners):
        id_copies[r].wait_recv()
        small = pltpu.make_async_copy(id_in.at[r], id_smem.at[r], small_sem.at[r])
        small.start()
        small.wait()
        locals_in.append(id_smem[r, 0, 0])
    for r in range(owners):
        id_tile[r * 16 : r * 16 + 16, :] = jnp.full(
            (16, LANES), locals_in[r].astype(jnp.float32), jnp.float32
        ).astype(jnp.bfloat16)

    def hops(direction, block):
        longer = replicas // 2
        first = block < owners // 2
        return longer if first == (direction == 0) else replicas - 1 - longer

    longest = replicas // 2
    peers = ((right, member), (left, member))
    id_moves = {}

    def send_ids(direction, hop):
        src = id_tile if hop == 1 else id_ring.at[direction, hop - 2]
        copy = remote(src, id_ring.at[direction, hop - 1], idr_sem.at[direction, hop - 1], peers[direction])
        copy.start()
        id_moves[direction, hop] = copy
        sent.append(copy)

    moves = {}

    def send_block(direction, hop, block):
        if hop > hops(direction, block):
            return
        src = hidden.at[block] if hop == 1 else ring.at[direction, hop - 2, block]
        copy = remote(
            src, ring.at[direction, hop - 1, block], ring_sem.at[direction, hop - 1, block],
            peers[direction],
        )
        copy.start()
        moves[direction, hop, block] = copy
        sent.append(copy)

    def add_gram(parts):
        kept = []
        for rows, ids in parts:
            match = (ids.astype(jnp.float32) == mine.astype(jnp.float32)).astype(jnp.float32)
            match = jnp.concatenate([match] * (width // LANES), axis=1)
            kept.append((rows.astype(jnp.float32) * match).astype(jnp.bfloat16))
        kept = jnp.concatenate(kept, axis=0)
        for at in range(0, width, LANES):
            gram_ref[at : at + LANES, at:] += lax.dot_general(
                kept[:, at : at + LANES], kept[:, at:], (((0,), (0,)), ((), ())),
                preferred_element_type=jnp.float32,
            )

    for direction in range(2):
        send_ids(direction, 1)
    gram_ref[...] = jnp.zeros_like(gram_ref)
    load_gate.wait()
    load_up.wait()

    queue = [(ready_time(b), 0, b) for b in range(owners)]
    order = []
    free = [0.0, 0.0]
    while queue:
        now, hop, b = heapq.heappop(queue)
        order.append((hop, b))
        landed = []
        for d in range(2):
            if hop < hops(d, b):
                free[d] = max(now, free[d]) + 2.0
                landed.append(free[d])
        if landed:
            heapq.heappush(queue, (max(landed), hop + 1, b))

    for hop, b in order:
        if hop == 0:
            if b > 0:
                token_copies[b].wait_recv()
                rows_in = arrived[b]
            else:
                rows_in = tokens_ref[picks[0][0]]
            which = jnp.maximum(locals_in[b], 0)
            gate = jnp.dot(rows_in, gate_w[which], preferred_element_type=jnp.float32)
            up = jnp.dot(rows_in, up_w[which], preferred_element_type=jnp.float32)
            hidden[b] = (gate / (1.0 + jnp.exp(-gate)) * up).astype(jnp.bfloat16)
            for d in range(2):
                send_block(d, 1, b)
            add_gram([(hidden[b], id_tile[b * 16 : b * 16 + 1, :])])
        else:
            parts = []
            for d in range(2):
                if hop > hops(d, b):
                    continue
                if (d, hop) in id_moves:
                    id_moves.pop((d, hop)).wait_recv()
                    if hop < longest:
                        send_ids(d, hop + 1)
                moves[d, hop, b].wait_recv()
                send_block(d, hop + 1, b)
                parts.append((d, hop - 1))
            add_gram([(ring[d, h, b], id_ring[d, h, b * 16 : b * 16 + 1, :]) for d, h in parts])
    for copy in sent:
        copy.wait_send()
    row = lax.broadcasted_iota(jnp.int32, (width, width), 0)
    col = lax.broadcasted_iota(jnp.int32, (width, width), 1)
    gram_ref[...] = gram_ref[...] * scale + jnp.where(row == col, RIDGE, 0.0)


def grams(tokens, block_expert, gate_weight, up_weight):
    owners = lax.axis_size("expert")
    replicas = lax.axis_size("dp")
    experts, model, width = gate_weight.shape
    mean_rows = tokens.shape[0] * replicas // experts
    longest = replicas // 2
    bf16 = jnp.bfloat16
    vmem = pl.BlockSpec(memory_space=pltpu.VMEM)
    anywhere = pl.BlockSpec(memory_space=pl.ANY)
    dma = pltpu.SemaphoreType.DMA
    return pl.pallas_call(
        functools.partial(gram_kernel, owners, replicas, experts, 1.0 / mean_rows),
        out_shape=jax.ShapeDtypeStruct((width, width), jnp.float32),
        in_specs=[pl.BlockSpec(memory_space=pltpu.SMEM), anywhere, anywhere, anywhere],
        out_specs=vmem,
        scratch_shapes=[
            pltpu.VMEM((tokens.shape[0] // BLOCK, BLOCK, model), bf16),
            pltpu.VMEM((experts, model, width), bf16),
            pltpu.VMEM((experts, model, width), bf16),
            pltpu.VMEM((owners, BLOCK, model), bf16),
            pltpu.VMEM((owners, BLOCK, model), bf16),
            pltpu.VMEM((owners, 8, LANES), jnp.int32),
            pltpu.VMEM((owners, 8, LANES), jnp.int32),
            pltpu.SMEM((owners, 8, LANES), jnp.int32),
            pltpu.VMEM((owners * 16, LANES), bf16),
            pltpu.VMEM((2, longest, owners * 16, LANES), bf16),
            pltpu.VMEM((owners, BLOCK, width), bf16),
            pltpu.VMEM((2, longest, owners, BLOCK, width), bf16),
            dma((3,)),
            dma((owners, 2)),
            dma((owners, 2)),
            dma((owners,)),
            dma((2, longest, owners, 2)),
            dma((2, longest, 2)),
        ],
        compiler_params=pltpu.CompilerParams(
            collective_id=0, has_side_effects=True, vmem_limit_bytes=52 * 1024 * 1024
        ),
        name="grams",
    )(block_expert, tokens.reshape(-1, BLOCK, model), gate_weight, up_weight)


def eliminate(tile, rows_done):
    size = tile.shape[0]
    count = size // PANEL
    halves = tile.shape[1] // LANES

    def spread(vector, lane):
        return jnp.broadcast_to(vector[:, lane : lane + 1], (PANEL, LANES))

    def down(vector, sub):
        return jnp.broadcast_to(vector[sub : sub + 1, :], (PANEL, LANES))

    groups = [
        [tile[g * PANEL : (g + 1) * PANEL, h * LANES : (h + 1) * LANES] for h in range(halves)]
        for g in range(count)
    ]
    for p in range(count):
        panel = groups[p]
        cols = [spread(panel[0], p * PANEL + k) for k in range(PANEL)]
        small = [[down(cols[k], i) if i >= k else None for k in range(PANEL)] for i in range(PANEL)]
        inverse = []
        low = [[None] * PANEL for _ in range(PANEL)]
        for k in range(PANEL):
            inv = lax.rsqrt(small[k][k])
            inverse.append(inv)
            for i in range(k + 1, PANEL):
                low[i][k] = small[i][k] * inv
            for i in range(k + 1, PANEL):
                for m in range(k + 1, i + 1):
                    small[i][m] = small[i][m] - low[i][k] * low[m][k]
        rows = []
        for k in range(PANEL):
            parts = []
            for h in range(halves):
                value = down(panel[h], k)
                for m in range(k):
                    value = value - low[k][m] * rows[m][h]
                parts.append(value * inverse[k])
            rows.append(parts)
            for h in range(halves):
                rows_done[p * PANEL + k : p * PANEL + k + 1, h * LANES : (h + 1) * LANES] = parts[h][0:1, :]
        for g in range(p + 1, count):
            weights = []
            for k in range(PANEL):
                value = spread(groups[g][0], p * PANEL + k)
                for m in range(k):
                    value = value - low[k][m] * weights[m]
                weights.append(value * inverse[k])
            for h in range(halves):
                value = groups[g][h]
                for k in range(PANEL):
                    value = value - weights[k] * rows[k][h]
                groups[g][h] = value


def factor_kernel(gram_ref, factor_ref, work, tile, done):
    width = gram_ref.shape[0]
    work[...] = gram_ref[...]
    row = lax.broadcasted_iota(jnp.int32, (LANES, LANES), 0)
    col = lax.broadcasted_iota(jnp.int32, (LANES, LANES), 1)

    def step(b, carry):
        at = pl.ds(pl.multiple_of(b * LANES, LANES), LANES)
        tile[:, :LANES] = work[at, at]
        tile[:, LANES:] = jnp.where(row == col, 1.0, 0.0)
        eliminate(tile, done)
        wide = jnp.dot(
            done[:, LANES:], work[at, :], precision=HIGHEST, preferred_element_type=jnp.float32
        )
        across = lax.broadcasted_iota(jnp.int32, wide.shape, 1) - b * LANES
        factor_ref[at, :] = jnp.where(across >= LANES, wide, 0.0)
        factor_ref[at, at] = jnp.where(row <= col, done[:, :LANES], 0.0)

        @pl.when(b + 1 < width // LANES)
        def _():
            work[...] -= lax.dot_general(
                wide, wide, (((0,), (0,)), ((), ())), precision=HIGHEST,
                preferred_element_type=jnp.float32,
            )

        return carry

    lax.fori_loop(0, width // LANES, step, 0)


def factored(gram):
    width = gram.shape[0]
    vmem = pl.BlockSpec(memory_space=pltpu.VMEM)
    return pl.pallas_call(
        factor_kernel,
        out_shape=jax.ShapeDtypeStruct((width, width), jnp.float32),
        in_specs=[vmem],
        out_specs=vmem,
        scratch_shapes=[
            pltpu.VMEM((width, width), jnp.float32),
            pltpu.VMEM((LANES, 2 * LANES), jnp.float32),
            pltpu.VMEM((LANES, 2 * LANES), jnp.float32),
        ],
        compiler_params=pltpu.CompilerParams(vmem_limit_bytes=16 * 1024 * 1024),
        name="factored",
    )(gram)


def spread_kernel(replicas, copies, factor_ref, out_ref, landed, sems):
    dp = lax.axis_index("dp")
    member = lax.axis_index("expert")
    rows = out_ref.shape[1]
    barrier = pltpu.get_barrier_semaphore()
    offsets = list(range(copies, replicas, copies))
    for r in offsets:
        pl.semaphore_signal(
            barrier, inc=1, device_id=((dp + r) % replicas, member), device_id_type=MESH
        )
    pl.semaphore_wait(barrier, len(offsets))
    sent = []
    for n, r in enumerate(offsets):
        to = (dp + r) % replicas
        copy = pltpu.make_async_remote_copy(
            src_ref=factor_ref.at[pl.ds(pl.multiple_of(to * rows, 8), rows), :],
            dst_ref=landed.at[n],
            send_sem=sems.at[n, 0],
            recv_sem=sems.at[n, 1],
            device_id=(to, member),
            device_id_type=MESH,
        )
        copy.start()
        sent.append(copy)
    out_ref[dp // copies] = factor_ref[pl.ds(pl.multiple_of(dp * rows, 8), rows), :]
    for n, r in enumerate(offsets):
        sent[n].wait_recv()
        origin = (dp + replicas - r) % replicas
        out_ref[origin // copies] = landed[n]
    for copy in sent:
        copy.wait_send()


def spread_rows(factor, experts):
    replicas = lax.axis_size("dp")
    copies = replicas // experts
    width = factor.shape[0]
    rows = width // replicas
    vmem = pl.BlockSpec(memory_space=pltpu.VMEM)
    return pl.pallas_call(
        functools.partial(spread_kernel, replicas, copies),
        out_shape=jax.ShapeDtypeStruct((experts, rows, width), jnp.float32),
        in_specs=[vmem],
        out_specs=vmem,
        scratch_shapes=[
            pltpu.VMEM((experts - 1, rows, width), jnp.float32),
            pltpu.SemaphoreType.DMA((experts - 1, 2)),
        ],
        compiler_params=pltpu.CompilerParams(
            collective_id=1, has_side_effects=True, vmem_limit_bytes=16 * 1024 * 1024
        ),
        name="spread_rows",
    )(factor)


def on_device(tokens, block_expert, gate_weight, up_weight):
    gram = grams(tokens, block_expert, gate_weight, up_weight)
    return spread_rows(factored(gram), gate_weight.shape[0])


def solution(mesh):
    placed = (
        P(("dp", "expert"), None),
        P(("dp", "expert")),
        P("expert", None, None),
        P("expert", None, None),
    )
    return jax.shard_map(
        on_device, mesh=mesh, in_specs=placed, out_specs=P("expert", "dp", None), check_vma=False
    )
```

```python
import functools
import heapq

import jax
import jax.numpy as jnp
from jax import lax
from jax.experimental import pallas as pl
from jax.experimental.pallas import tpu as pltpu
from jax.sharding import PartitionSpec as P

BLOCK = 128
RIDGE = 0.05
PANEL = 8
LANES = 128
MESH = pl.DeviceIdType.MESH
HIGHEST = lax.Precision.HIGHEST


def flip(index, bits, count):
    out = 0
    bit = 1
    while bit < count:
        digit = (index // bit) % 2
        out = out + bit * ((digit + 1) % 2 if bits & bit else digit)
        bit *= 2
    return out


def ready_time(block):
    return (0.0, 0.7, 6.0, 7.5)[block] if block < 4 else 2.0 * block


def ring_place(dp, count):
    row, side = dp // 2, dp % 2
    return row + side * (count - 1 - 2 * row)


def ring_index(place, count):
    late = place // (count // 2)
    return (1 - late) * 2 * place + late * (2 * (count - 1 - place) + 1)


def gram_kernel(
    owners, replicas, experts, scale,
    expert_ref, tokens_hbm, gate_hbm, up_hbm, gram_ref,
    tokens_ref, gate_w, up_w, outgoing, arrived, id_out, id_in, id_smem, id_tile, id_ring,
    hidden, ring, w_sem, tok_sem, id_sem, small_sem, ring_sem, idr_sem,
):
    dp = lax.axis_index("dp")
    member = lax.axis_index("expert")
    width = gram_ref.shape[0]
    blocks_dev = expert_ref.shape[0]
    place = ring_place(dp, replicas)
    right = ring_index((place + 1) % replicas, replicas)
    left = ring_index((place + replicas - 1) % replicas, replicas)
    mine = dp // max(1, replicas // experts)

    load_gate = pltpu.make_async_copy(gate_hbm, gate_w, w_sem.at[0])
    load_up = pltpu.make_async_copy(up_hbm, up_w, w_sem.at[1])
    load_tokens = pltpu.make_async_copy(tokens_hbm, tokens_ref, w_sem.at[2])
    load_tokens.start()
    load_gate.start()
    load_up.start()

    barrier = pltpu.get_barrier_semaphore()
    for r in range(1, owners):
        pl.semaphore_signal(
            barrier, inc=1, device_id=(dp, flip(member, r, owners)), device_id_type=MESH
        )
    for side in (left, right):
        pl.semaphore_signal(barrier, inc=1, device_id=(side, member), device_id_type=MESH)

    picks = []
    for r in range(owners):
        target = flip(member, r, owners)
        index = jnp.int32(0)
        local = jnp.int32(-1)
        for b in range(blocks_dev):
            named = expert_ref[b]
            hit = named // experts == target
            index = jnp.where(hit, b, index)
            local = jnp.where(hit, named % experts, local)
        picks.append((index, local))
        id_out[r] = jnp.full((8, LANES), local, jnp.int32)
    pl.semaphore_wait(barrier, owners + 1)

    def remote(src, dst, sems, device):
        return pltpu.make_async_remote_copy(
            src_ref=src, dst_ref=dst, send_sem=sems.at[0], recv_sem=sems.at[1],
            device_id=device, device_id_type=MESH,
        )

    sent = []
    id_copies = [None]
    for r in range(1, owners):
        device = (dp, flip(member, r, owners))
        copy = remote(id_out.at[r], id_in.at[r], id_sem.at[r], device)
        copy.start()
        id_copies.append(copy)
        sent.append(copy)
    load_tokens.wait()
    token_copies = [None] * owners
    for r in list(range(2, owners)) + [1]:
        device = (dp, flip(member, r, owners))
        outgoing[r] = tokens_ref[picks[r][0]]
        copy = remote(outgoing.at[r], arrived.at[r], tok_sem.at[r], device)
        copy.start()
        token_copies[r] = copy
        sent.append(copy)

    locals_in = [picks[0][1]]

    def keep_id(r):
        id_tile[r * 16 : r * 16 + 16, :] = jnp.full(
            (16, LANES), locals_in[r].astype(jnp.float32), jnp.float32
        ).astype(jnp.bfloat16)

    def collect_ids():
        small = [None]
        for r in range(1, owners):
            id_copies[r].wait_recv()
            small.append(pltpu.make_async_copy(id_in.at[r], id_smem.at[r], small_sem.at[r]))
            small[r].start()
        for r in range(1, owners):
            small[r].wait()
            locals_in.append(id_smem[r, 0, 0])
            keep_id(r)

    keep_id(0)
    def hops(direction, block):
        longer = replicas // 2
        first = block < owners // 2
        return longer if first == (direction == 0) else replicas - 1 - longer

    longest = replicas // 2
    peers = ((right, member), (left, member))
    id_moves = {}

    def send_ids(direction, hop):
        src = id_tile if hop == 1 else id_ring.at[direction, hop - 2]
        copy = remote(src, id_ring.at[direction, hop - 1], idr_sem.at[direction, hop - 1], peers[direction])
        copy.start()
        id_moves[direction, hop] = copy
        sent.append(copy)

    moves = {}

    def send_block(direction, hop, block):
        if hop > hops(direction, block):
            return
        src = hidden.at[block] if hop == 1 else ring.at[direction, hop - 2, block]
        copy = remote(
            src, ring.at[direction, hop - 1, block], ring_sem.at[direction, hop - 1, block],
            peers[direction],
        )
        copy.start()
        moves[direction, hop, block] = copy
        sent.append(copy)

    def add_gram(parts):
        kept = []
        for rows, ids in parts:
            match = (ids.astype(jnp.float32) == mine.astype(jnp.float32)).astype(jnp.float32)
            match = jnp.concatenate([match] * (width // LANES), axis=1)
            kept.append((rows.astype(jnp.float32) * match).astype(jnp.bfloat16))
        kept = jnp.concatenate(kept, axis=0)
        for at in range(0, width, LANES):
            gram_ref[at : at + LANES, at:] += lax.dot_general(
                kept[:, at : at + LANES], kept[:, at:], (((0,), (0,)), ((), ())),
                preferred_element_type=jnp.float32,
            )

    gram_ref[...] = jnp.zeros_like(gram_ref)

    queue = [(ready_time(b), 0, b) for b in range(owners)]
    order = []
    free = [0.0, 0.0]
    while queue:
        now, hop, b = heapq.heappop(queue)
        order.append((hop, b))
        landed = []
        for d in range(2):
            if hop < hops(d, b):
                free[d] = max(now, free[d]) + 2.0
                landed.append(free[d])
        if landed:
            heapq.heappush(queue, (max(landed), hop + 1, b))

    for hop, b in order:
        if hop == 0:
            if b > 0:
                token_copies[b].wait_recv()
                rows_in = arrived[b]
            else:
                rows_in = tokens_ref[picks[0][0]]
            which = jnp.maximum(locals_in[b], 0)
            if b == 0:
                load_gate.wait()
            gate = jnp.dot(rows_in, gate_w[which], preferred_element_type=jnp.float32)
            if b == 0:
                load_up.wait()
            up = jnp.dot(rows_in, up_w[which], preferred_element_type=jnp.float32)
            hidden[b] = (gate / (1.0 + jnp.exp(-gate)) * up).astype(jnp.bfloat16)
            for d in range(2):
                send_block(d, 1, b)
            if b == 0:
                collect_ids()
                for d in range(2):
                    send_ids(d, 1)
            add_gram([(hidden[b], id_tile[b * 16 : b * 16 + 1, :])])
        else:
            parts = []
            for d in range(2):
                if hop > hops(d, b):
                    continue
                if (d, hop) in id_moves:
                    id_moves.pop((d, hop)).wait_recv()
                    if hop < longest:
                        send_ids(d, hop + 1)
                moves[d, hop, b].wait_recv()
                send_block(d, hop + 1, b)
                parts.append((d, hop - 1))
            add_gram([(ring[d, h, b], id_ring[d, h, b * 16 : b * 16 + 1, :]) for d, h in parts])
    for copy in sent:
        copy.wait_send()
    row = lax.broadcasted_iota(jnp.int32, (width, width), 0)
    col = lax.broadcasted_iota(jnp.int32, (width, width), 1)
    gram_ref[...] = gram_ref[...] * scale + jnp.where(row == col, RIDGE, 0.0)


def grams(tokens, block_expert, gate_weight, up_weight):
    owners = lax.axis_size("expert")
    replicas = lax.axis_size("dp")
    experts, model, width = gate_weight.shape
    mean_rows = tokens.shape[0] * replicas // experts
    longest = replicas // 2
    bf16 = jnp.bfloat16
    vmem = pl.BlockSpec(memory_space=pltpu.VMEM)
    anywhere = pl.BlockSpec(memory_space=pl.ANY)
    dma = pltpu.SemaphoreType.DMA
    return pl.pallas_call(
        functools.partial(gram_kernel, owners, replicas, experts, 1.0 / mean_rows),
        out_shape=jax.ShapeDtypeStruct((width, width), jnp.float32),
        in_specs=[pl.BlockSpec(memory_space=pltpu.SMEM), anywhere, anywhere, anywhere],
        out_specs=vmem,
        scratch_shapes=[
            pltpu.VMEM((tokens.shape[0] // BLOCK, BLOCK, model), bf16),
            pltpu.VMEM((experts, model, width), bf16),
            pltpu.VMEM((experts, model, width), bf16),
            pltpu.VMEM((owners, BLOCK, model), bf16),
            pltpu.VMEM((owners, BLOCK, model), bf16),
            pltpu.VMEM((owners, 8, LANES), jnp.int32),
            pltpu.VMEM((owners, 8, LANES), jnp.int32),
            pltpu.SMEM((owners, 8, LANES), jnp.int32),
            pltpu.VMEM((owners * 16, LANES), bf16),
            pltpu.VMEM((2, longest, owners * 16, LANES), bf16),
            pltpu.VMEM((owners, BLOCK, width), bf16),
            pltpu.VMEM((2, longest, owners, BLOCK, width), bf16),
            dma((3,)),
            dma((owners, 2)),
            dma((owners, 2)),
            dma((owners,)),
            dma((2, longest, owners, 2)),
            dma((2, longest, 2)),
        ],
        compiler_params=pltpu.CompilerParams(
            collective_id=0, has_side_effects=True, vmem_limit_bytes=52 * 1024 * 1024
        ),
        name="grams",
    )(block_expert, tokens.reshape(-1, BLOCK, model), gate_weight, up_weight)


def eliminate(tile, rows_done):
    size = tile.shape[0]
    count = size // PANEL
    halves = tile.shape[1] // LANES

    def spread(vector, lane):
        return jnp.broadcast_to(vector[:, lane : lane + 1], (PANEL, LANES))

    def down(vector, sub):
        return jnp.broadcast_to(vector[sub : sub + 1, :], (PANEL, LANES))

    groups = [
        [tile[g * PANEL : (g + 1) * PANEL, h * LANES : (h + 1) * LANES] for h in range(halves)]
        for g in range(count)
    ]
    for p in range(count):
        panel = groups[p]
        cols = [spread(panel[0], p * PANEL + k) for k in range(PANEL)]
        small = [[down(cols[k], i) if i >= k else None for k in range(PANEL)] for i in range(PANEL)]
        inverse = []
        low = [[None] * PANEL for _ in range(PANEL)]
        for k in range(PANEL):
            inv = lax.rsqrt(small[k][k])
            inverse.append(inv)
            for i in range(k + 1, PANEL):
                low[i][k] = small[i][k] * inv
            for i in range(k + 1, PANEL):
                for m in range(k + 1, i + 1):
                    small[i][m] = small[i][m] - low[i][k] * low[m][k]
        rows = []
        for k in range(PANEL):
            parts = []
            for h in range(halves):
                value = down(panel[h], k)
                for m in range(k):
                    value = value - low[k][m] * rows[m][h]
                parts.append(value * inverse[k])
            rows.append(parts)
            for h in range(halves):
                rows_done[p * PANEL + k : p * PANEL + k + 1, h * LANES : (h + 1) * LANES] = parts[h][0:1, :]
        for g in range(p + 1, count):
            weights = []
            for k in range(PANEL):
                value = spread(groups[g][0], p * PANEL + k)
                for m in range(k):
                    value = value - low[k][m] * weights[m]
                weights.append(value * inverse[k])
            for h in range(halves):
                value = groups[g][h]
                for k in range(PANEL):
                    value = value - weights[k] * rows[k][h]
                groups[g][h] = value


def factor_kernel(gram_ref, rows_ref, factor_ref, work, tile, done):
    width = gram_ref.shape[0]
    work[...] = gram_ref[...]
    row = lax.broadcasted_iota(jnp.int32, (LANES, LANES), 0)
    col = lax.broadcasted_iota(jnp.int32, (LANES, LANES), 1)

    def step(b, carry):
        at = pl.ds(pl.multiple_of(b * LANES, LANES), LANES)
        tile[:, :LANES] = work[at, at]
        tile[:, LANES:] = jnp.where(row == col, 1.0, 0.0)
        eliminate(tile, done)
        wide = jnp.dot(
            done[:, LANES:], work[at, :], precision=HIGHEST, preferred_element_type=jnp.float32
        )
        across = lax.broadcasted_iota(jnp.int32, wide.shape, 1) - b * LANES
        factor_ref[at, :] = jnp.where(across >= LANES, wide, 0.0)
        factor_ref[at, at] = jnp.where(row <= col, done[:, :LANES], 0.0)

        @pl.when(b + 1 < width // LANES)
        def _():
            work[...] -= lax.dot_general(
                wide, wide, (((0,), (0,)), ((), ())), precision=HIGHEST,
                preferred_element_type=jnp.float32,
            )

        return carry

    lax.fori_loop(0, width // LANES, step, 0)
    replicas, padded, _ = rows_ref.shape
    rows = width // replicas
    for d in range(replicas):
        part = factor_ref[d * rows : (d + 1) * rows, :]
        if padded > rows:
            part = jnp.concatenate([part, jnp.zeros((padded - rows, width), part.dtype)], axis=0)
        rows_ref[d] = part.astype(rows_ref.dtype)


def factored(gram, replicas):
    width = gram.shape[0]
    padded = -(-(width // replicas) // 16) * 16
    vmem = pl.BlockSpec(memory_space=pltpu.VMEM)
    return pl.pallas_call(
        factor_kernel,
        out_shape=jax.ShapeDtypeStruct((replicas, padded, width), jnp.bfloat16),
        in_specs=[vmem],
        out_specs=vmem,
        scratch_shapes=[
            pltpu.VMEM((width, width), jnp.float32),
            pltpu.VMEM((width, width), jnp.float32),
            pltpu.VMEM((LANES, 2 * LANES), jnp.float32),
            pltpu.VMEM((LANES, 2 * LANES), jnp.float32),
        ],
        compiler_params=pltpu.CompilerParams(vmem_limit_bytes=16 * 1024 * 1024),
        name="factored",
    )(gram)


def spread_kernel(replicas, copies, factor_ref, out_ref, landed, sems):
    dp = lax.axis_index("dp")
    member = lax.axis_index("expert")
    barrier = pltpu.get_barrier_semaphore()
    offsets = list(range(copies, replicas, copies))
    for r in offsets:
        pl.semaphore_signal(
            barrier, inc=1, device_id=((dp + r) % replicas, member), device_id_type=MESH
        )
    pl.semaphore_wait(barrier, len(offsets))
    sent = []
    for n, r in enumerate(offsets):
        to = (dp + r) % replicas
        copy = pltpu.make_async_remote_copy(
            src_ref=factor_ref.at[to],
            dst_ref=landed.at[n],
            send_sem=sems.at[n, 0],
            recv_sem=sems.at[n, 1],
            device_id=(to, member),
            device_id_type=MESH,
        )
        copy.start()
        sent.append(copy)
    out_ref[dp // copies] = factor_ref[dp]
    for n, r in enumerate(offsets):
        sent[n].wait_recv()
        origin = (dp + replicas - r) % replicas
        out_ref[origin // copies] = landed[n]
    for copy in sent:
        copy.wait_send()


def spread_rows(factor, experts):
    replicas, padded, width = factor.shape
    rows = width // replicas
    vmem = pl.BlockSpec(memory_space=pltpu.VMEM)
    out = pl.pallas_call(
        functools.partial(spread_kernel, replicas, replicas // experts),
        out_shape=jax.ShapeDtypeStruct((experts, padded, width), factor.dtype),
        in_specs=[vmem],
        out_specs=vmem,
        scratch_shapes=[
            pltpu.VMEM((experts - 1, padded, width), factor.dtype),
            pltpu.SemaphoreType.DMA((experts - 1, 2)),
        ],
        compiler_params=pltpu.CompilerParams(
            collective_id=1, has_side_effects=True, vmem_limit_bytes=16 * 1024 * 1024
        ),
        name="spread_rows",
    )(factor)
    return out[:, :rows].astype(jnp.float32)


def on_device(tokens, block_expert, gate_weight, up_weight):
    gram = grams(tokens, block_expert, gate_weight, up_weight)
    return spread_rows(factored(gram, lax.axis_size("dp")), gate_weight.shape[0])


def solution(mesh):
    placed = (
        P(("dp", "expert"), None),
        P(("dp", "expert")),
        P("expert", None, None),
        P("expert", None, None),
    )
    return jax.shard_map(
        on_device, mesh=mesh, in_specs=placed, out_specs=P("expert", "dp", None), check_vma=False
    )
```

```python
import functools
import heapq

import jax
import jax.numpy as jnp
from jax import lax
from jax.experimental import pallas as pl
from jax.experimental.pallas import tpu as pltpu
from jax.sharding import PartitionSpec as P

BLOCK = 128
RIDGE = 0.05
PANEL = 8
LANES = 128
MESH = pl.DeviceIdType.MESH
HIGHEST = lax.Precision.HIGHEST


def flip(index, bits, count):
    out = 0
    bit = 1
    while bit < count:
        digit = (index // bit) % 2
        out = out + bit * ((digit + 1) % 2 if bits & bit else digit)
        bit *= 2
    return out


def ready_time(block):
    return (0.0, 0.7, 6.0, 7.5)[block] if block < 4 else 2.0 * block


def ring_place(dp, count):
    row, side = dp // 2, dp % 2
    return row + side * (count - 1 - 2 * row)


def ring_index(place, count):
    late = place // (count // 2)
    return (1 - late) * 2 * place + late * (2 * (count - 1 - place) + 1)


def gram_kernel(
    owners, replicas, experts, scale,
    expert_ref, tokens_hbm, gate_hbm, up_hbm, gram_ref,
    tokens_ref, gate_w, up_w, outgoing, arrived, id_out, id_in, id_smem, id_tile, id_ring,
    hidden, ring, w_sem, tok_sem, id_sem, small_sem, ring_sem, idr_sem,
):
    dp = lax.axis_index("dp")
    member = lax.axis_index("expert")
    width = gram_ref.shape[0]
    blocks_dev = expert_ref.shape[0]
    place = ring_place(dp, replicas)
    right = ring_index((place + 1) % replicas, replicas)
    left = ring_index((place + replicas - 1) % replicas, replicas)
    mine = dp // max(1, replicas // experts)

    load_gate = pltpu.make_async_copy(gate_hbm, gate_w, w_sem.at[0])
    load_up = pltpu.make_async_copy(up_hbm, up_w, w_sem.at[1])
    load_tokens = pltpu.make_async_copy(tokens_hbm, tokens_ref, w_sem.at[2])
    load_tokens.start()
    load_gate.start()
    load_up.start()

    barrier = pltpu.get_barrier_semaphore()
    for r in range(1, owners):
        pl.semaphore_signal(
            barrier, inc=1, device_id=(dp, flip(member, r, owners)), device_id_type=MESH
        )
    for side in (left, right):
        pl.semaphore_signal(barrier, inc=1, device_id=(side, member), device_id_type=MESH)

    picks = []
    for r in range(owners):
        target = flip(member, r, owners)
        index = jnp.int32(0)
        local = jnp.int32(-1)
        for b in range(blocks_dev):
            named = expert_ref[b]
            hit = named // experts == target
            index = jnp.where(hit, b, index)
            local = jnp.where(hit, named % experts, local)
        picks.append((index, local))
        id_out[r] = jnp.full((8, LANES), local, jnp.int32)
    pl.semaphore_wait(barrier, owners + 1)

    def remote(src, dst, sems, device):
        return pltpu.make_async_remote_copy(
            src_ref=src, dst_ref=dst, send_sem=sems.at[0], recv_sem=sems.at[1],
            device_id=device, device_id_type=MESH,
        )

    sent = []
    id_copies = [None]
    for r in range(1, owners):
        device = (dp, flip(member, r, owners))
        copy = remote(id_out.at[r], id_in.at[r], id_sem.at[r], device)
        copy.start()
        id_copies.append(copy)
        sent.append(copy)
    load_tokens.wait()
    token_copies = [None] * owners
    for r in list(range(2, owners)) + [1]:
        device = (dp, flip(member, r, owners))
        outgoing[r] = tokens_ref[picks[r][0]]
        copy = remote(outgoing.at[r], arrived.at[r], tok_sem.at[r], device)
        copy.start()
        token_copies[r] = copy
        sent.append(copy)

    locals_in = [picks[0][1]]

    def keep_id(r):
        id_tile[r * 16 : r * 16 + 16, :] = jnp.full(
            (16, LANES), locals_in[r].astype(jnp.float32), jnp.float32
        ).astype(jnp.bfloat16)

    def collect_ids():
        small = [None]
        for r in range(1, owners):
            id_copies[r].wait_recv()
            small.append(pltpu.make_async_copy(id_in.at[r], id_smem.at[r], small_sem.at[r]))
            small[r].start()
        for r in range(1, owners):
            small[r].wait()
            locals_in.append(id_smem[r, 0, 0])
            keep_id(r)

    keep_id(0)
    def hops(direction, block):
        longer = replicas // 2
        first = block < owners // 2
        return longer if first == (direction == 0) else replicas - 1 - longer

    longest = replicas // 2
    peers = ((right, member), (left, member))
    id_moves = {}

    def send_ids(direction, hop):
        src = id_tile if hop == 1 else id_ring.at[direction, hop - 2]
        copy = remote(src, id_ring.at[direction, hop - 1], idr_sem.at[direction, hop - 1], peers[direction])
        copy.start()
        id_moves[direction, hop] = copy
        sent.append(copy)

    moves = {}

    def send_block(direction, hop, block):
        if hop > hops(direction, block):
            return
        src = hidden.at[block] if hop == 1 else ring.at[direction, hop - 2, block]
        copy = remote(
            src, ring.at[direction, hop - 1, block], ring_sem.at[direction, hop - 1, block],
            peers[direction],
        )
        copy.start()
        moves[direction, hop, block] = copy
        sent.append(copy)

    def add_gram(parts):
        kept = []
        for rows, ids in parts:
            match = (ids.astype(jnp.float32) == mine.astype(jnp.float32)).astype(jnp.float32)
            match = jnp.concatenate([match] * (width // LANES), axis=1)
            kept.append((rows.astype(jnp.float32) * match).astype(jnp.bfloat16))
        kept = jnp.concatenate(kept, axis=0)
        for at in range(0, width, LANES):
            gram_ref[at : at + LANES, at:] += lax.dot_general(
                kept[:, at : at + LANES], kept[:, at:], (((0,), (0,)), ((), ())),
                preferred_element_type=jnp.float32,
            )

    gram_ref[...] = jnp.zeros_like(gram_ref)

    queue = [(ready_time(b), 0, b) for b in range(owners)]
    order = []
    free = [0.0, 0.0]
    while queue:
        now, hop, b = heapq.heappop(queue)
        order.append((hop, b))
        landed = []
        for d in range(2):
            if hop < hops(d, b):
                free[d] = max(now, free[d]) + 2.0
                landed.append(free[d])
        if landed:
            heapq.heappush(queue, (max(landed), hop + 1, b))

    for hop, b in order:
        if hop == 0:
            if b > 0:
                token_copies[b].wait_recv()
                rows_in = arrived[b]
            else:
                rows_in = tokens_ref[picks[0][0]]
            which = jnp.maximum(locals_in[b], 0)
            if b == 0:
                load_gate.wait()
            gate = jnp.dot(rows_in, gate_w[which], preferred_element_type=jnp.float32)
            if b == 0:
                load_up.wait()
            up = jnp.dot(rows_in, up_w[which], preferred_element_type=jnp.float32)
            hidden[b] = (gate / (1.0 + jnp.exp(-gate)) * up).astype(jnp.bfloat16)
            for d in range(2):
                send_block(d, 1, b)
            if b == 0:
                collect_ids()
                for d in range(2):
                    send_ids(d, 1)
            add_gram([(hidden[b], id_tile[b * 16 : b * 16 + 1, :])])
        else:
            parts = []
            for d in range(2):
                if hop > hops(d, b):
                    continue
                if (d, hop) in id_moves:
                    id_moves.pop((d, hop)).wait_recv()
                    if hop < longest:
                        send_ids(d, hop + 1)
                moves[d, hop, b].wait_recv()
                send_block(d, hop + 1, b)
                parts.append((d, hop - 1))
            add_gram([(ring[d, h, b], id_ring[d, h, b * 16 : b * 16 + 1, :]) for d, h in parts])
    for copy in sent:
        copy.wait_send()
    row = lax.broadcasted_iota(jnp.int32, (width, width), 0)
    col = lax.broadcasted_iota(jnp.int32, (width, width), 1)
    gram_ref[...] = gram_ref[...] * scale + jnp.where(row == col, RIDGE, 0.0)


def grams(tokens, block_expert, gate_weight, up_weight):
    owners = lax.axis_size("expert")
    replicas = lax.axis_size("dp")
    experts, model, width = gate_weight.shape
    mean_rows = tokens.shape[0] * replicas // experts
    longest = replicas // 2
    bf16 = jnp.bfloat16
    vmem = pl.BlockSpec(memory_space=pltpu.VMEM)
    anywhere = pl.BlockSpec(memory_space=pl.ANY)
    dma = pltpu.SemaphoreType.DMA
    return pl.pallas_call(
        functools.partial(gram_kernel, owners, replicas, experts, 1.0 / mean_rows),
        out_shape=jax.ShapeDtypeStruct((width, width), jnp.float32),
        in_specs=[pl.BlockSpec(memory_space=pltpu.SMEM), anywhere, anywhere, anywhere],
        out_specs=vmem,
        scratch_shapes=[
            pltpu.VMEM((tokens.shape[0] // BLOCK, BLOCK, model), bf16),
            pltpu.VMEM((experts, model, width), bf16),
            pltpu.VMEM((experts, model, width), bf16),
            pltpu.VMEM((owners, BLOCK, model), bf16),
            pltpu.VMEM((owners, BLOCK, model), bf16),
            pltpu.VMEM((owners, 8, LANES), jnp.int32),
            pltpu.VMEM((owners, 8, LANES), jnp.int32),
            pltpu.SMEM((owners, 8, LANES), jnp.int32),
            pltpu.VMEM((owners * 16, LANES), bf16),
            pltpu.VMEM((2, longest, owners * 16, LANES), bf16),
            pltpu.VMEM((owners, BLOCK, width), bf16),
            pltpu.VMEM((2, longest, owners, BLOCK, width), bf16),
            dma((3,)),
            dma((owners, 2)),
            dma((owners, 2)),
            dma((owners,)),
            dma((2, longest, owners, 2)),
            dma((2, longest, 2)),
        ],
        compiler_params=pltpu.CompilerParams(
            collective_id=0, has_side_effects=True, vmem_limit_bytes=52 * 1024 * 1024
        ),
        name="grams",
    )(block_expert, tokens.reshape(-1, BLOCK, model), gate_weight, up_weight)


def eliminate(tile, rows_done):
    size = tile.shape[0]
    count = size // PANEL
    halves = tile.shape[1] // LANES

    def spread(vector, lane):
        return jnp.broadcast_to(vector[:, lane : lane + 1], (PANEL, LANES))

    def down(vector, sub):
        return jnp.broadcast_to(vector[sub : sub + 1, :], (PANEL, LANES))

    groups = [
        [tile[g * PANEL : (g + 1) * PANEL, h * LANES : (h + 1) * LANES] for h in range(halves)]
        for g in range(count)
    ]
    for p in range(count):
        panel = groups[p]
        cols = [spread(panel[0], p * PANEL + k) for k in range(PANEL)]
        small = [[down(cols[k], i) if i >= k else None for k in range(PANEL)] for i in range(PANEL)]
        inverse = []
        low = [[None] * PANEL for _ in range(PANEL)]
        for k in range(PANEL):
            inv = lax.rsqrt(small[k][k])
            inverse.append(inv)
            for i in range(k + 1, PANEL):
                low[i][k] = small[i][k] * inv
            for i in range(k + 1, PANEL):
                for m in range(k + 1, i + 1):
                    small[i][m] = small[i][m] - low[i][k] * low[m][k]
        rows = []
        for k in range(PANEL):
            parts = []
            for h in range(halves):
                value = down(panel[h], k)
                for m in range(k):
                    value = value - low[k][m] * rows[m][h]
                parts.append(value * inverse[k])
            rows.append(parts)
            for h in range(halves):
                rows_done[p * PANEL + k : p * PANEL + k + 1, h * LANES : (h + 1) * LANES] = parts[h][0:1, :]
        for g in range(p + 1, count):
            weights = []
            for k in range(PANEL):
                value = spread(groups[g][0], p * PANEL + k)
                for m in range(k):
                    value = value - low[k][m] * weights[m]
                weights.append(value * inverse[k])
            for h in range(halves):
                value = groups[g][h]
                for k in range(PANEL):
                    value = value - weights[k] * rows[k][h]
                groups[g][h] = value


def row_pieces(width, rows):
    pieces = []
    for holder in range(width // rows):
        start, end, which = holder * rows, (holder + 1) * rows, 0
        while start < end:
            stop = min(end, (start // LANES + 1) * LANES)
            pieces.append((start // LANES, holder, start, stop, which))
            start, which = stop, which + 1
    return pieces


def factor_kernel(replicas, copies, gram_ref, out_ref, factor, work, tile, done, landed, send_sem, recv_sem):
    dp = lax.axis_index("dp")
    member = lax.axis_index("expert")
    width = gram_ref.shape[0]
    rows = width // replicas
    pieces = row_pieces(width, rows)

    barrier = pltpu.get_barrier_semaphore()
    offsets = list(range(copies, replicas, copies))
    for r in offsets:
        pl.semaphore_signal(
            barrier, inc=1, device_id=((dp + r) % replicas, member), device_id_type=MESH
        )

    def piece_copy(block, holder, start, stop, which, origin):
        first = start - holder * rows
        return pltpu.make_async_remote_copy(
            src_ref=factor.at[start:stop, block * LANES :],
            dst_ref=landed.at[origin, first : first + stop - start, block * LANES :],
            send_sem=send_sem.at[holder, which],
            recv_sem=recv_sem.at[origin, which],
            device_id=(holder, member),
            device_id_type=MESH,
        )

    def serves(holder):
        return jnp.logical_and(dp % copies == holder % copies, dp != holder)

    work[...] = gram_ref[...]
    out_ref[...] = jnp.zeros_like(out_ref)
    row = lax.broadcasted_iota(jnp.int32, (LANES, LANES), 0)
    col = lax.broadcasted_iota(jnp.int32, (LANES, LANES), 1)
    pl.semaphore_wait(barrier, len(offsets))

    def step(b, carry):
        at = pl.ds(pl.multiple_of(b * LANES, LANES), LANES)
        tile[:, :LANES] = work[at, at]
        tile[:, LANES:] = jnp.where(row == col, 1.0, 0.0)
        eliminate(tile, done)
        wide = jnp.dot(
            done[:, LANES:], work[at, :], precision=HIGHEST, preferred_element_type=jnp.float32
        )
        across = lax.broadcasted_iota(jnp.int32, wide.shape, 1) - b * LANES
        factor[at, :] = jnp.where(across >= LANES, wide, 0.0)
        factor[at, at] = jnp.where(row <= col, done[:, :LANES], 0.0)
        for piece in pieces:

            @pl.when(jnp.logical_and(b == piece[0], serves(piece[1])))
            def _():
                piece_copy(*piece, dp // copies).start()

        @pl.when(b + 1 < width // LANES)
        def _():
            work[...] -= lax.dot_general(
                wide, wide, (((0,), (0,)), ((), ())), precision=HIGHEST,
                preferred_element_type=jnp.float32,
            )

        return carry

    lax.fori_loop(0, width // LANES, step, 0)

    out_ref[dp // copies] = factor[pl.ds(pl.multiple_of(dp * rows, 8), rows), :]
    for piece in pieces:
        block, holder, start, stop, which = piece
        first = start - holder * rows

        @pl.when(dp == holder)
        def _():
            for origin in range(replicas // copies):
                if origin != holder // copies:
                    piece_copy(*piece, origin).wait_recv()
                    part = (origin, slice(first, first + stop - start), slice(block * LANES, width))
                    out_ref[part] = landed[part]

    for piece in pieces:

        @pl.when(serves(piece[1]))
        def _():
            piece_copy(*piece, dp // copies).wait_send()


def factored_rows(gram, experts):
    width = gram.shape[0]
    replicas = lax.axis_size("dp")
    rows = width // replicas
    most = 1 + max(piece[4] for piece in row_pieces(width, rows))
    vmem = pl.BlockSpec(memory_space=pltpu.VMEM)
    return pl.pallas_call(
        functools.partial(factor_kernel, replicas, replicas // experts),
        out_shape=jax.ShapeDtypeStruct((experts, rows, width), jnp.float32),
        in_specs=[vmem],
        out_specs=vmem,
        scratch_shapes=[
            pltpu.VMEM((width, width), jnp.float32),
            pltpu.VMEM((width, width), jnp.float32),
            pltpu.VMEM((LANES, 2 * LANES), jnp.float32),
            pltpu.VMEM((LANES, 2 * LANES), jnp.float32),
            pltpu.VMEM((experts, rows, width), jnp.float32),
            pltpu.SemaphoreType.DMA((replicas, most)),
            pltpu.SemaphoreType.DMA((experts, most)),
        ],
        compiler_params=pltpu.CompilerParams(
            collective_id=1, has_side_effects=True, vmem_limit_bytes=16 * 1024 * 1024
        ),
        name="factored_rows",
    )(gram)


def on_device(tokens, block_expert, gate_weight, up_weight):
    gram = grams(tokens, block_expert, gate_weight, up_weight)
    return factored_rows(gram, gate_weight.shape[0])


def solution(mesh):
    placed = (
        P(("dp", "expert"), None),
        P(("dp", "expert")),
        P("expert", None, None),
        P("expert", None, None),
    )
    return jax.shard_map(
        on_device, mesh=mesh, in_specs=placed, out_specs=P("expert", "dp", None), check_vma=False
    )
```

```python
import functools
import heapq

import jax
import jax.numpy as jnp
from jax import lax
from jax.experimental import pallas as pl
from jax.experimental.pallas import tpu as pltpu
from jax.sharding import PartitionSpec as P

BLOCK = 128
RIDGE = 0.05
PANEL = 8
LANES = 128
MESH = pl.DeviceIdType.MESH
HIGHEST = lax.Precision.HIGHEST


def flip(index, bits, count):
    out = 0
    bit = 1
    while bit < count:
        digit = (index // bit) % 2
        out = out + bit * ((digit + 1) % 2 if bits & bit else digit)
        bit *= 2
    return out


def ready_time(block):
    return (0.0, 0.7, 9.0, 10.0)[block] if block < 4 else 2.0 * block


def ring_place(dp, count):
    row, side = dp // 2, dp % 2
    return row + side * (count - 1 - 2 * row)


def ring_index(place, count):
    late = place // (count // 2)
    return (1 - late) * 2 * place + late * (2 * (count - 1 - place) + 1)


def gram_kernel(
    owners, replicas, experts, scale,
    expert_ref, tokens_hbm, gate_hbm, up_hbm, gram_ref,
    tokens_ref, gate_w, up_w, outgoing, arrived, id_out, id_in, id_smem, id_tile, id_ring,
    hidden, ring, w_sem, tok_sem, id_sem, small_sem, ring_sem, idr_sem,
):
    dp = lax.axis_index("dp")
    member = lax.axis_index("expert")
    width = gram_ref.shape[0]
    blocks_dev = expert_ref.shape[0]
    place = ring_place(dp, replicas)
    right = ring_index((place + 1) % replicas, replicas)
    left = ring_index((place + replicas - 1) % replicas, replicas)
    mine = dp // max(1, replicas // experts)

    load_gate = pltpu.make_async_copy(gate_hbm, gate_w, w_sem.at[0])
    load_up = pltpu.make_async_copy(up_hbm, up_w, w_sem.at[1])
    load_tokens = pltpu.make_async_copy(tokens_hbm, tokens_ref, w_sem.at[2])
    load_tokens.start()
    load_gate.start()
    load_up.start()

    barrier = pltpu.get_barrier_semaphore()
    for r in range(1, owners):
        pl.semaphore_signal(
            barrier, inc=1, device_id=(dp, flip(member, r, owners)), device_id_type=MESH
        )
    for side in (left, right):
        pl.semaphore_signal(barrier, inc=1, device_id=(side, member), device_id_type=MESH)

    picks = []
    for r in range(owners):
        target = flip(member, r, owners)
        index = jnp.int32(0)
        local = jnp.int32(-1)
        for b in range(blocks_dev):
            named = expert_ref[b]
            hit = named // experts == target
            index = jnp.where(hit, b, index)
            local = jnp.where(hit, named % experts, local)
        picks.append((index, local))
        id_out[r] = jnp.full((8, LANES), local, jnp.int32)
    pl.semaphore_wait(barrier, owners + 1)

    def remote(src, dst, sems, device):
        return pltpu.make_async_remote_copy(
            src_ref=src, dst_ref=dst, send_sem=sems.at[0], recv_sem=sems.at[1],
            device_id=device, device_id_type=MESH,
        )

    sent = []
    id_copies = [None]
    for r in range(1, owners):
        device = (dp, flip(member, r, owners))
        copy = remote(id_out.at[r], id_in.at[r], id_sem.at[r], device)
        copy.start()
        id_copies.append(copy)
        sent.append(copy)
    load_tokens.wait()
    token_copies = [None] * owners
    for r in list(range(2, owners)) + [1]:
        device = (dp, flip(member, r, owners))
        outgoing[r] = tokens_ref[picks[r][0]]
        copy = remote(outgoing.at[r], arrived.at[r], tok_sem.at[r], device)
        copy.start()
        token_copies[r] = copy
        sent.append(copy)

    locals_in = [picks[0][1]]

    sub = lax.broadcasted_iota(jnp.int32, (16, LANES), 0)

    def keep_ids():
        table = jnp.full((16, LANES), -1.0, jnp.float32)
        for r in range(owners):
            table = jnp.where(sub == r, locals_in[r].astype(jnp.float32), table)
        id_tile[...] = table.astype(jnp.bfloat16)

    def collect_ids():
        small = [None]
        for r in range(1, owners):
            id_copies[r].wait_recv()
            small.append(pltpu.make_async_copy(id_in.at[r], id_smem.at[r], small_sem.at[r]))
            small[r].start()
        for r in range(1, owners):
            small[r].wait()
            locals_in.append(id_smem[r, 0, 0])
        keep_ids()

    def hops(direction, block):
        longer = replicas // 2
        first = block < owners // 2
        return longer if first == (direction == 0) else replicas - 1 - longer

    longest = replicas // 2
    peers = ((right, member), (left, member))
    id_moves = {}

    def send_ids(direction, hop):
        src = id_tile if hop == 1 else id_ring.at[direction, hop - 2]
        copy = remote(src, id_ring.at[direction, hop - 1], idr_sem.at[direction, hop - 1], peers[direction])
        copy.start()
        id_moves[direction, hop] = copy
        sent.append(copy)

    moves = {}

    def send_block(direction, hop, block):
        if hop > hops(direction, block):
            return
        src = hidden.at[block] if hop == 1 else ring.at[direction, hop - 2, block]
        copy = remote(
            src, ring.at[direction, hop - 1, block], ring_sem.at[direction, hop - 1, block],
            peers[direction],
        )
        copy.start()
        moves[direction, hop, block] = copy
        sent.append(copy)

    def add_gram(parts):
        kept = []
        for rows, table, b in parts:
            ids = table.astype(jnp.float32)[b : b + 1, :]
            match = (ids == mine.astype(jnp.float32)).astype(jnp.float32)
            match = jnp.concatenate([match] * (width // LANES), axis=1)
            kept.append((rows.astype(jnp.float32) * match).astype(jnp.bfloat16))
        kept = jnp.concatenate(kept, axis=0)
        for at in range(0, width, LANES):
            gram_ref[at : at + LANES, at:] += lax.dot_general(
                kept[:, at : at + LANES], kept[:, at:], (((0,), (0,)), ((), ())),
                preferred_element_type=jnp.float32,
            )

    gram_ref[...] = jnp.zeros_like(gram_ref)

    queue = [(ready_time(b), 0, b) for b in range(owners)]
    order = []
    free = [0.0, 0.0]
    while queue:
        now, hop, b = heapq.heappop(queue)
        order.append((hop, b))
        landed = []
        for d in range(2):
            if hop < hops(d, b):
                free[d] = max(now, free[d]) + 2.0
                landed.append(free[d])
        if landed:
            heapq.heappush(queue, (max(landed), hop + 1, b))

    for hop, b in order:
        if hop == 0:
            if b > 0:
                token_copies[b].wait_recv()
                rows_in = arrived[b]
            else:
                rows_in = tokens_ref[picks[0][0]]
            which = jnp.maximum(locals_in[b], 0)
            if b == 0:
                load_gate.wait()
            gate = jnp.dot(rows_in, gate_w[which], preferred_element_type=jnp.float32)
            if b == 0:
                load_up.wait()
            up = jnp.dot(rows_in, up_w[which], preferred_element_type=jnp.float32)
            hidden[b] = (gate / (1.0 + jnp.exp(-gate)) * up).astype(jnp.bfloat16)
            for d in range(2):
                send_block(d, 1, b)
            if b == 0:
                collect_ids()
                for d in range(2):
                    send_ids(d, 1)
            add_gram([(hidden[b], id_tile[...], b)])
        else:
            parts = []
            for d in range(2):
                if hop > hops(d, b):
                    continue
                if (d, hop) in id_moves:
                    id_moves.pop((d, hop)).wait_recv()
                    if hop < longest:
                        send_ids(d, hop + 1)
                moves[d, hop, b].wait_recv()
                send_block(d, hop + 1, b)
                parts.append((d, hop - 1))
            add_gram([(ring[d, h, b], id_ring[d, h], b) for d, h in parts])
    for copy in sent:
        copy.wait_send()
    row = lax.broadcasted_iota(jnp.int32, (width, width), 0)
    col = lax.broadcasted_iota(jnp.int32, (width, width), 1)
    gram_ref[...] = gram_ref[...] * scale + jnp.where(row == col, RIDGE, 0.0)


def grams(tokens, block_expert, gate_weight, up_weight):
    owners = lax.axis_size("expert")
    replicas = lax.axis_size("dp")
    experts, model, width = gate_weight.shape
    mean_rows = tokens.shape[0] * replicas // experts
    longest = replicas // 2
    bf16 = jnp.bfloat16
    vmem = pl.BlockSpec(memory_space=pltpu.VMEM)
    anywhere = pl.BlockSpec(memory_space=pl.ANY)
    dma = pltpu.SemaphoreType.DMA
    return pl.pallas_call(
        functools.partial(gram_kernel, owners, replicas, experts, 1.0 / mean_rows),
        out_shape=jax.ShapeDtypeStruct((width, width), jnp.float32),
        in_specs=[pl.BlockSpec(memory_space=pltpu.SMEM), anywhere, anywhere, anywhere],
        out_specs=vmem,
        scratch_shapes=[
            pltpu.VMEM((tokens.shape[0] // BLOCK, BLOCK, model), bf16),
            pltpu.VMEM((experts, model, width), bf16),
            pltpu.VMEM((experts, model, width), bf16),
            pltpu.VMEM((owners, BLOCK, model), bf16),
            pltpu.VMEM((owners, BLOCK, model), bf16),
            pltpu.VMEM((owners, 8, LANES), jnp.int32),
            pltpu.VMEM((owners, 8, LANES), jnp.int32),
            pltpu.SMEM((owners, 8, LANES), jnp.int32),
            pltpu.VMEM((16, LANES), bf16),
            pltpu.VMEM((2, longest, 16, LANES), bf16),
            pltpu.VMEM((owners, BLOCK, width), bf16),
            pltpu.VMEM((2, longest, owners, BLOCK, width), bf16),
            dma((3,)),
            dma((owners, 2)),
            dma((owners, 2)),
            dma((owners,)),
            dma((2, longest, owners, 2)),
            dma((2, longest, 2)),
        ],
        compiler_params=pltpu.CompilerParams(
            collective_id=0, has_side_effects=True, vmem_limit_bytes=60 * 1024 * 1024
        ),
        name="grams",
    )(block_expert, tokens.reshape(-1, BLOCK, model), gate_weight, up_weight)


def eliminate(tile, rows_done):
    size = tile.shape[0]
    count = size // PANEL
    halves = tile.shape[1] // LANES

    def spread(vector, lane):
        return jnp.broadcast_to(vector[:, lane : lane + 1], (PANEL, LANES))

    def down(vector, sub):
        return jnp.broadcast_to(vector[sub : sub + 1, :], (PANEL, LANES))

    groups = [
        [tile[g * PANEL : (g + 1) * PANEL, h * LANES : (h + 1) * LANES] for h in range(halves)]
        for g in range(count)
    ]
    for p in range(count):
        panel = groups[p]
        cols = [spread(panel[0], p * PANEL + k) for k in range(PANEL)]
        small = [[down(cols[k], i) if i >= k else None for k in range(PANEL)] for i in range(PANEL)]
        inverse = []
        low = [[None] * PANEL for _ in range(PANEL)]
        for k in range(PANEL):
            inv = lax.rsqrt(small[k][k])
            inverse.append(inv)
            for i in range(k + 1, PANEL):
                low[i][k] = small[i][k] * inv
            for i in range(k + 1, PANEL):
                for m in range(k + 1, i + 1):
                    small[i][m] = small[i][m] - low[i][k] * low[m][k]
        rows = []
        for k in range(PANEL):
            parts = []
            for h in range(halves):
                value = down(panel[h], k)
                for m in range(k):
                    value = value - low[k][m] * rows[m][h]
                parts.append(value * inverse[k])
            rows.append(parts)
            for h in range(halves):
                rows_done[p * PANEL + k : p * PANEL + k + 1, h * LANES : (h + 1) * LANES] = parts[h][0:1, :]
        for g in range(p + 1, count):
            weights = []
            for k in range(PANEL):
                value = spread(groups[g][0], p * PANEL + k)
                for m in range(k):
                    value = value - low[k][m] * weights[m]
                weights.append(value * inverse[k])
            for h in range(halves):
                value = groups[g][h]
                for k in range(PANEL):
                    value = value - weights[k] * rows[k][h]
                groups[g][h] = value


def row_pieces(width, rows):
    pieces = []
    for holder in range(width // rows):
        start, end, which = holder * rows, (holder + 1) * rows, 0
        while start < end:
            stop = min(end, (start // LANES + 1) * LANES)
            pieces.append((start // LANES, holder, start, stop, which))
            start, which = stop, which + 1
    return pieces


def factor_kernel(replicas, copies, gram_ref, out_ref, factor, work, tile, done, landed, send_sem, recv_sem):
    dp = lax.axis_index("dp")
    member = lax.axis_index("expert")
    width = gram_ref.shape[0]
    rows = width // replicas
    pieces = row_pieces(width, rows)

    barrier = pltpu.get_barrier_semaphore()
    offsets = list(range(copies, replicas, copies))
    for r in offsets:
        pl.semaphore_signal(
            barrier, inc=1, device_id=((dp + r) % replicas, member), device_id_type=MESH
        )

    def piece_copy(block, holder, start, stop, which, origin):
        first = start - holder * rows
        return pltpu.make_async_remote_copy(
            src_ref=factor.at[start:stop, block * LANES :],
            dst_ref=landed.at[origin, first : first + stop - start, block * LANES :],
            send_sem=send_sem.at[holder, which],
            recv_sem=recv_sem.at[origin, which],
            device_id=(holder, member),
            device_id_type=MESH,
        )

    def serves(holder):
        return jnp.logical_and(dp % copies == holder % copies, dp != holder)

    work[...] = gram_ref[...]
    out_ref[...] = jnp.zeros_like(out_ref)
    row = lax.broadcasted_iota(jnp.int32, (LANES, LANES), 0)
    col = lax.broadcasted_iota(jnp.int32, (LANES, LANES), 1)
    pl.semaphore_wait(barrier, len(offsets))

    def step(b, carry):
        at = pl.ds(pl.multiple_of(b * LANES, LANES), LANES)
        tile[:, :LANES] = work[at, at]
        tile[:, LANES:] = jnp.where(row == col, 1.0, 0.0)
        eliminate(tile, done)
        wide = jnp.dot(
            done[:, LANES:], work[at, :], precision=HIGHEST, preferred_element_type=jnp.float32
        )
        across = lax.broadcasted_iota(jnp.int32, wide.shape, 1) - b * LANES
        factor[at, :] = jnp.where(across >= LANES, wide, 0.0)
        factor[at, at] = jnp.where(row <= col, done[:, :LANES], 0.0)
        for piece in pieces:

            @pl.when(jnp.logical_and(b == piece[0], serves(piece[1])))
            def _():
                piece_copy(*piece, dp // copies).start()

        @pl.when(b + 1 < width // LANES)
        def _():
            work[...] -= lax.dot_general(
                wide, wide, (((0,), (0,)), ((), ())), precision=HIGHEST,
                preferred_element_type=jnp.float32,
            )

        return carry

    lax.fori_loop(0, width // LANES, step, 0)

    out_ref[dp // copies] = factor[pl.ds(pl.multiple_of(dp * rows, 8), rows), :]
    for piece in pieces:
        block, holder, start, stop, which = piece
        first = start - holder * rows

        @pl.when(dp == holder)
        def _():
            for origin in range(replicas // copies):
                if origin != holder // copies:
                    piece_copy(*piece, origin).wait_recv()
                    part = (origin, slice(first, first + stop - start), slice(block * LANES, width))
                    out_ref[part] = landed[part]

    for piece in pieces:

        @pl.when(serves(piece[1]))
        def _():
            piece_copy(*piece, dp // copies).wait_send()


def factored_rows(gram, experts):
    width = gram.shape[0]
    replicas = lax.axis_size("dp")
    rows = width // replicas
    most = 1 + max(piece[4] for piece in row_pieces(width, rows))
    vmem = pl.BlockSpec(memory_space=pltpu.VMEM)
    return pl.pallas_call(
        functools.partial(factor_kernel, replicas, replicas // experts),
        out_shape=jax.ShapeDtypeStruct((experts, rows, width), jnp.float32),
        in_specs=[vmem],
        out_specs=vmem,
        scratch_shapes=[
            pltpu.VMEM((width, width), jnp.float32),
            pltpu.VMEM((width, width), jnp.float32),
            pltpu.VMEM((LANES, 2 * LANES), jnp.float32),
            pltpu.VMEM((LANES, 2 * LANES), jnp.float32),
            pltpu.VMEM((experts, rows, width), jnp.float32),
            pltpu.SemaphoreType.DMA((replicas, most)),
            pltpu.SemaphoreType.DMA((experts, most)),
        ],
        compiler_params=pltpu.CompilerParams(
            collective_id=1, has_side_effects=True, vmem_limit_bytes=16 * 1024 * 1024
        ),
        name="factored_rows",
    )(gram)


def on_device(tokens, block_expert, gate_weight, up_weight):
    gram = grams(tokens, block_expert, gate_weight, up_weight)
    return factored_rows(gram, gate_weight.shape[0])


def solution(mesh):
    placed = (
        P(("dp", "expert"), None),
        P(("dp", "expert")),
        P("expert", None, None),
        P("expert", None, None),
    )
    return jax.shard_map(
        on_device, mesh=mesh, in_specs=placed, out_specs=P("expert", "dp", None), check_vma=False
    )
```
